32 devices in a mesh: groups: 1, pair: 8 (over z, core), vir: 4 (over y, x).
Axes of the slice: x: 2, y: 2, z: 4, core: 2. Of those that a mesh axis runs over, the one named last changes fastest.
Arguments:
- amplitudes: bfloat16 [8, 2560, 2560], P(('groups', 'pair'), 'vir'), may hold values from -6 to 6
- ladder_factor: bfloat16 [1, 20, 4, 128, 128], P('groups'), may hold values from -0.25 to 0.25
- ladder_tiles: int32 [20, 4], P('groups'), may hold values from 0 to 19, as said below
- cycle_integrals: bfloat16 [80, 4, 128, 128], P(('groups', 'pair')), may hold values from -0.25 to 0.25
- cycle_tiles: int32 [80, 4], P('groups'), may hold values from 0 to 79, as said below
- cycle_slots: int32 [80], P('groups'), may hold values from 0 to 79, as said below
- slab_order: int32 [8], P('groups'), may hold values from 0 to 7, each once
- amp_mask: int32 [8, 20, 20], P(('groups', 'pair'), 'vir'), may hold values 0 or 1
Outputs:
- residual: bfloat16 [8, 2560, 2560], P(('groups', 'pair'), 'vir')
The draws below stay inside these ranges and needn't reach their ends.
Inputs may be any that keep to these rules, and one draw needn't show every extreme that they name: `ladder_tiles`: row t names 4 different tiles, the first of them t itself. `cycle_tiles`: row t names 4 different tiles, the first of them t itself. `cycle_slots`: different column tiles have different slots.
All inputs are finite; a program needn't handle non-finite values. No bound on the sum of `amp_mask` on one device may be relied on, other than what follows from the above.
Results may differ from the reference program's by a relative error of at most 0.0051.
Values may be sent and summed in bfloat16 or wider, within the bound.
A program may use at most 192 MiB of HBM per device.

```python
import jax
import jax.numpy as jnp
from jax import lax

TILE = 128
NV = 2560
NJ = 4
KB = 4
KW = 4
NQ = 1
NT = 20
PAIRS = 8
NCT = 80
SLOTS = 80


def neighbour_table(key, count, kept_count):
    row_keys = jax.random.split(key, count)

    def one_row(row_key, row_index):
        shuffle = jax.random.permutation(row_key, count - 1).astype(jnp.int32)
        others = (row_index + 1 + shuffle[:kept_count - 1]) % count
        return jnp.concatenate([row_index[None], others]).astype(jnp.int32)
    return jax.vmap(one_row)(row_keys, jnp.arange(count, dtype=jnp.int32))


def draw_ladder_tiles(key, part):
    key = jax.random.fold_in(key, 11)
    return neighbour_table(key, NT, KB)


def draw_cycle_tiles(key, part):
    key = jax.random.fold_in(key, 12)
    return neighbour_table(key, NCT, KW)


def draw_cycle_slots(key, part):
    key = jax.random.fold_in(key, 13)
    first_key, second_key = jax.random.split(key)
    middle = jax.random.permutation(first_key, SLOTS - 2)[:NCT - 2].astype(jnp.int32) + 1
    extremes = jnp.array([0, SLOTS - 1], jnp.int32)
    joined = jnp.concatenate([middle, extremes])
    return joined[jax.random.permutation(second_key, NCT)].astype(jnp.int32)


def set_ends(entries, rng, low, top_value):
    dims = entries.shape
    place = [jax.random.randint(jax.random.fold_in(rng, axis), (), 0, dims[axis]) for axis in range(len(dims))]
    entries = entries.at[tuple(place)].set(low)
    longest = dims.index(max(dims))
    place[longest] = (place[longest] + 1) % dims[longest]
    return entries.at[tuple(place)].set(top_value)


def block_levels(key, extent, cuts, low, top_value):
    def one(dim, blocks):
        draws = jax.random.uniform(jax.random.fold_in(jax.random.fold_in(key, 6), dim), (blocks,), jnp.float32, low / len(cuts), top_value / len(cuts))
        return jnp.repeat(jnp.exp(draws), extent[dim] // blocks).reshape((-1,) + (1,) * (len(extent) - dim - 1))

    factor_of = one(*cuts[0])
    for cut in cuts[1:]:
        factor_of = factor_of * one(*cut)
    return factor_of


def centred(rng, extent, width, bound, pieces=(), kind=jnp.bfloat16):
    drawn = jax.random.normal(rng, extent, jnp.float32) * width
    if len(pieces) > 0:
        drawn = block_levels(rng, extent, pieces, -0.22, 0.18) * drawn
    return jnp.clip(drawn, min=-bound, max=bound).astype(kind)


def setup_inputs(seed: int = 0, part: int = 0) -> dict:
    seeds = jax.random.split(jax.random.key(seed), 9)
    part_splits = jax.random.split(jax.random.fold_in(seeds[8], part), 9)
    amplitudes = centred(part_splits[0], (PAIRS, NV, NV), 1.0, 6.0, ((0, 8), (1, 4)))
    ladder_factor = centred(part_splits[1], (NQ, NT, KB, TILE, TILE), (KB * TILE) ** -0.5, 0.25)
    ladder_tiles = draw_ladder_tiles(jax.random.fold_in(jax.random.fold_in(seeds[8], part), 71), part)
    cycle_integrals = centred(part_splits[3], (SLOTS, KW, TILE, TILE), (KW * TILE) ** -0.5, 0.25, ((0, 8),))
    cycle_tiles = draw_cycle_tiles(jax.random.fold_in(jax.random.fold_in(seeds[8], part), 71), part)
    cycle_slots = draw_cycle_slots(jax.random.fold_in(jax.random.fold_in(seeds[8], part), 71), part)
    slab_order = jax.random.permutation(part_splits[6], PAIRS).astype(jnp.int32)
    amp_mask = set_ends((jax.random.randint(part_splits[7], (PAIRS, NT, NT), 0, 4) < 3).astype(jnp.int32), jax.random.fold_in(part_splits[7], 1), 0, 1)
    return {"amplitudes": amplitudes, "ladder_factor": ladder_factor, "ladder_tiles": ladder_tiles, "cycle_integrals": cycle_integrals, "cycle_tiles": cycle_tiles, "cycle_slots": cycle_slots, "slab_order": slab_order, "amp_mask": amp_mask}


def reference(amplitudes, ladder_factor, ladder_tiles, cycle_integrals, cycle_tiles, cycle_slots, slab_order, amp_mask):
    pair_count = amplitudes.shape[0]
    outer_count = pair_count // NJ
    col_tiles = NJ * NT
    positions = jnp.arange(pair_count, dtype=jnp.int32)
    inverse = jnp.zeros((pair_count,), jnp.int32).at[slab_order].set(positions)
    pair_grid = jnp.take(amplitudes, inverse, axis=0)
    left_rows = pair_grid.reshape(outer_count, NJ, NV, NV).transpose(0, 2, 1, 3).reshape(outer_count * NV, col_tiles, TILE)
    integrals = jnp.take(cycle_integrals, cycle_slots, axis=0).astype(jnp.float32)

    def one_column(column_index):
        piece_rows = jnp.take(left_rows, cycle_tiles[column_index], axis=1).astype(jnp.float32)
        return jnp.einsum("rkc,kcb->rb", piece_rows, integrals[column_index]).astype(jnp.bfloat16)

    cycle_term = lax.map(one_column, jnp.arange(col_tiles, dtype=jnp.int32))
    cycle_term = cycle_term.reshape(NJ, NT, outer_count, NV, TILE).transpose(2, 0, 3, 1, 4).reshape(pair_count, NV, NV)
    cycle_rows = jnp.take(cycle_term, slab_order, axis=0)
    factors = ladder_factor.astype(jnp.float32)

    def finish(pair_items):
        amp_pair, cycle_pair, mask_pair = pair_items
        blocks = amp_pair.reshape(NT, TILE, NV)
        picked = jnp.take(blocks, ladder_tiles, axis=0).astype(jnp.float32)
        summed = jnp.zeros((NV, NT, TILE), jnp.float32)
        for vector in range(NQ):
            inner_term = jnp.einsum("tkac,tkcd->tad", factors[vector], picked).astype(jnp.bfloat16)
            chosen = jnp.take(inner_term.reshape(NV, NT, TILE), ladder_tiles, axis=1).astype(jnp.float32)
            summed = summed + jnp.einsum("rtkd,tkbd->rtb", chosen, factors[vector])
        summed = summed.reshape(NV, NV) + cycle_pair.astype(jnp.float32)
        masked = summed.reshape(NT, TILE, NT, TILE) * mask_pair.astype(jnp.float32)[:, None, :, None]
        return masked.reshape(NV, NV).astype(jnp.bfloat16)

    return lax.map(finish, (amplitudes, cycle_rows, amp_mask))
```

```python
import functools

import jax
import jax.numpy as jnp
from jax import lax
from jax.experimental import pallas as pl
from jax.experimental.pallas import tpu as pltpu
from jax.sharding import PartitionSpec as P

NJ = 4
CORES = 2
MESH = pl.DeviceIdType.MESH


def kernel(
    pair_count,
    vir_count,
    ladder_tiles,
    cycle_tiles,
    cycle_slots,
    slab_order,
    inverse,
    amplitudes,
    amplitude_rows,
    factor,
    own_integrals,
    mask_rows,
    out,
    pair_rows,
    row_tiles,
    integrals,
    columns,
    inner_out,
    inner_in,
    cycle_out,
    cycle_in,
    ladder_sum,
    local_sem,
    pair_sem,
    back_sem,
    vir_sem,
    inner_sem,
    near_sem,
    share_sem,
    core_sem,
):
    pair = lax.axis_index("pair")
    vir = lax.axis_index("vir")
    tile = factor.shape[-1]
    kept = factor.shape[1]
    kept_cycle = own_integrals.shape[1]
    tile_count = factor.shape[0]
    local_tiles = amplitudes.shape[0]
    row_count = local_tiles * tile
    sub_rows = pair_rows.shape[1]
    own_slots = own_integrals.shape[0]
    layer_count = pair_count // CORES
    layer = pair // CORES
    core = pair % CORES
    other_core = layer * CORES + (1 - core)

    def remote(src, dst, sems, index, device):
        return pltpu.make_async_remote_copy(
            src_ref=src,
            dst_ref=dst,
            send_sem=sems.at[0, index],
            recv_sem=sems.at[1, index],
            device_id=device,
            device_id_type=MESH,
        )

    def rows_of(index):
        return pl.ds(pl.multiple_of(index * sub_rows, 16), sub_rows)

    def block_of(index):
        return pl.ds(pl.multiple_of(index * row_count, tile), row_count)

    def tile_at(index):
        return pl.ds(pl.multiple_of(index * tile, tile), tile)

    def slots_of(index):
        return pl.ds(index * own_slots, own_slots)

    def tiles_of(index):
        return pl.ds(index * local_tiles, local_tiles)

    barrier = pltpu.get_barrier_semaphore()
    for step in range(1, pair_count):
        pl.semaphore_signal(
            barrier, inc=1, device_id={"pair": (pair + step) % pair_count}, device_id_type=MESH
        )
    for step in range(1, vir_count):
        pl.semaphore_signal(
            barrier, inc=1, device_id={"vir": (vir + step) % vir_count}, device_id_type=MESH
        )
    pl.semaphore_wait(barrier, pair_count + vir_count - 2)

    near = []
    for step in range(1, layer_count):
        peer = ((layer + step) % layer_count) * CORES + core
        copy = remote(
            own_integrals.at[:, vir],
            integrals.at[slots_of(pair), vir],
            near_sem,
            step,
            {"pair": peer},
        )
        copy.start()
        near.append(copy)
    crossing = []
    for step in range(1, vir_count):
        peer = (vir + step) % vir_count
        copy = remote(
            amplitudes.at[:, :, block_of(peer)],
            columns.at[tiles_of(vir)],
            vir_sem,
            step,
            {"vir": peer},
        )
        copy.start()
        crossing.append(copy)
    order = sorted(range(1, pair_count), key=lambda step: -min(step, pair_count - step))
    forward = []
    for step in order:
        peer = (pair + step) % pair_count
        copy = remote(
            amplitude_rows.at[rows_of(peer), :], pair_rows.at[pair], pair_sem, step, {"pair": peer}
        )
        copy.start()
        forward.append(copy)
    local = [
        pltpu.make_async_copy(own_integrals, integrals.at[slots_of(pair)], local_sem.at[0]),
        pltpu.make_async_copy(
            amplitudes.at[:, :, block_of(vir)], columns.at[tiles_of(vir)], local_sem.at[1]
        ),
        pltpu.make_async_copy(
            amplitude_rows.at[rows_of(pair), :], pair_rows.at[pair], local_sem.at[2]
        ),
    ]
    for copy in local:
        copy.start()
    across = []
    copy = remote(
        own_integrals, integrals.at[slots_of(pair)], core_sem, 0, {"pair": other_core}
    )
    copy.start()
    across.append(copy)

    shared = []
    for step in range(1, layer_count):
        near[step - 1].wait_recv()
        source = ((layer + layer_count - step) % layer_count) * CORES + core
        for hop in range(1, vir_count):
            copy = remote(
                integrals.at[slots_of(source), vir],
                integrals.at[slots_of(source), vir],
                share_sem,
                step * vir_count + hop,
                {"vir": (vir + hop) % vir_count},
            )
            copy.start()
            shared.append(copy)

    for copy in crossing:
        copy.wait_recv()
    local[1].wait()

    def inner_step(owner, index):
        row_tile = owner * local_tiles + index
        left = jnp.concatenate([factor[row_tile, k] for k in range(kept)], axis=1)
        right = jnp.concatenate(
            [columns[ladder_tiles[row_tile, k]] for k in range(kept)], axis=0
        )
        value = jnp.dot(left, right, preferred_element_type=jnp.float32).astype(jnp.bfloat16)
        for part in range(local_tiles):
            inner_out[owner, part, tile_at(index), :] = value[:, part * tile : (part + 1) * tile]

    inner_sends = []
    for step in list(range(1, vir_count)) + [0]:
        peer = (vir + step) % vir_count

        @pl.loop(0, local_tiles)
        def _(index):
            inner_step(peer, index)

        if step:
            copy = remote(
                inner_out.at[peer], inner_in.at[tiles_of(vir)], inner_sem, step, {"vir": peer}
            )
            copy.start()
            inner_sends.append(copy)
        else:
            own_inner = pltpu.make_async_copy(
                inner_out.at[peer], inner_in.at[tiles_of(vir)], local_sem.at[3]
            )
            own_inner.start()

    for step in range(1, layer_count):
        for hop in range(1, vir_count):
            shared[(step - 1) * (vir_count - 1) + hop - 1].wait_recv()
        source = ((layer + layer_count - step) % layer_count) * CORES + core
        copy = remote(
            integrals.at[slots_of(source)],
            integrals.at[slots_of(source)],
            core_sem,
            step,
            {"pair": other_core},
        )
        copy.start()
        across.append(copy)

    def split_columns(source):
        for index in range(tile_count):
            row_tiles[source * tile_count + index] = pair_rows[
                source, :, index * tile : (index + 1) * tile
            ]

    local[0].wait()
    local[2].wait()
    split_columns(pair)
    for step, copy in zip(order, forward):
        copy.wait_recv()
        split_columns((pair + pair_count - step) % pair_count)
    for copy in across:
        copy.wait_recv()

    def cycle_step(peer, index):
        flat = slab_order[peer]
        outer = lax.div(flat, NJ)
        column = lax.rem(flat, NJ) * tile_count + index
        pieces = []
        for k in range(kept_cycle):
            row_tile = cycle_tiles[column, k]
            held = inverse[outer * NJ + lax.div(row_tile, tile_count)]
            pieces.append(row_tiles[held * tile_count + lax.rem(row_tile, tile_count)])
        left = jnp.concatenate(pieces, axis=1)
        right = integrals[cycle_slots[column]].reshape(kept_cycle * tile, tile)
        value = jnp.dot(left, right, preferred_element_type=jnp.float32)
        cycle_out[peer, :, tile_at(index)] = value.astype(jnp.bfloat16)

    back = []
    for step in order + [0]:
        peer = (pair + step) % pair_count

        @pl.loop(0, tile_count)
        def _(index):
            cycle_step(peer, index)

        if step:
            copy = remote(
                cycle_out.at[peer], cycle_in.at[rows_of(pair), :], back_sem, step, {"pair": peer}
            )
            copy.start()
            back.append(copy)
        else:
            own_back = pltpu.make_async_copy(
                cycle_out.at[peer], cycle_in.at[rows_of(pair), :], local_sem.at[4]
            )
            own_back.start()

    for copy in inner_sends:
        copy.wait_recv()
    own_inner.wait()

    @pl.loop(0, tile_count)
    def _(index):
        left = jnp.concatenate([inner_in[ladder_tiles[index, k]] for k in range(kept)], axis=1)
        right = jnp.concatenate([factor[index, k] for k in range(kept)], axis=1)
        ladder_sum[:, tile_at(index)] = lax.dot_general(
            left, right, (((1,), (1,)), ((), ())), preferred_element_type=jnp.float32
        )

    def finish(source):
        for part in range(sub_rows // 16):
            row = source * sub_rows + part * 16
            rows = pl.ds(pl.multiple_of(row, 16), 16)
            total = ladder_sum[rows, :] + cycle_in[rows, :].astype(jnp.float32)
            out[rows, :] = (mask_rows[pl.ds(row // tile, 1), :] * total).astype(jnp.bfloat16)

    own_back.wait()
    finish(pair)
    for step, copy in sorted(zip(order, back), key=lambda item: item[0] not in (1, 7)):
        copy.wait_recv()
        finish((pair + pair_count - step) % pair_count)
    for copy in near + crossing + forward + across + shared + inner_sends + back:
        copy.wait_send()


def fused(
    amplitudes,
    ladder_factor,
    ladder_tiles,
    cycle_integrals,
    cycle_tiles,
    cycle_slots,
    slab_order,
    amp_mask,
    pair_count,
    vir_count,
):
    tile = ladder_factor.shape[-1]
    _, row_count, full_width = amplitudes.shape
    tile_count = full_width // tile
    sub_rows = row_count // pair_count
    own_slots, kept_cycle = cycle_integrals.shape[:2]
    positions = jnp.arange(pair_count, dtype=jnp.int32)
    inverse = jnp.sum(
        jnp.where(slab_order[None, :] == positions[:, None], positions[None, :], 0), axis=1
    )
    mask_rows = jnp.repeat(amp_mask[0].astype(jnp.float32), tile, axis=1)
    smem = pl.BlockSpec(memory_space=pltpu.SMEM)
    vmem = pl.BlockSpec(memory_space=pltpu.VMEM)
    hbm = pl.BlockSpec(memory_space=pl.ANY)
    layer_count = pair_count // CORES

    def sems(count):
        return pltpu.SemaphoreType.DMA((2, count))

    result = pl.pallas_call(
        functools.partial(kernel, pair_count, vir_count),
        out_shape=jax.ShapeDtypeStruct((row_count, full_width), jnp.bfloat16),
        in_specs=[smem] * 5 + [hbm, hbm, vmem, hbm, vmem],
        out_specs=vmem,
        scratch_shapes=[
            pltpu.VMEM((pair_count, sub_rows, full_width), jnp.bfloat16),
            pltpu.VMEM((pair_count * tile_count, sub_rows, tile), jnp.bfloat16),
            pltpu.VMEM((own_slots * pair_count, kept_cycle, tile, tile), jnp.bfloat16),
            pltpu.VMEM((tile_count, tile, row_count), jnp.bfloat16),
            pltpu.VMEM((vir_count, row_count // tile, row_count, tile), jnp.bfloat16),
            pltpu.VMEM((tile_count, row_count, tile), jnp.bfloat16),
            pltpu.VMEM((pair_count, sub_rows, full_width), jnp.bfloat16),
            pltpu.VMEM((row_count, full_width), jnp.bfloat16),
            pltpu.VMEM((row_count, full_width), jnp.float32),
            pltpu.SemaphoreType.DMA((5,)),
            sems(pair_count),
            sems(pair_count),
            sems(vir_count),
            sems(vir_count),
            sems(layer_count),
            sems(layer_count * vir_count),
            sems(layer_count),
        ],
        compiler_params=pltpu.CompilerParams(
            collective_id=0, has_side_effects=True, vmem_limit_bytes=56 * 1024 * 1024
        ),
    )(
        ladder_tiles,
        cycle_tiles,
        cycle_slots,
        slab_order,
        inverse,
        amplitudes.reshape(row_count // tile, tile, full_width),
        amplitudes[0],
        ladder_factor[0],
        cycle_integrals,
        mask_rows,
    )
    return result[None]


def on_device(
    amplitudes,
    ladder_factor,
    ladder_tiles,
    cycle_integrals,
    cycle_tiles,
    cycle_slots,
    slab_order,
    amp_mask,
):
    tile_size = ladder_factor.shape[-1]
    row_count = amplitudes.shape[1]
    full_width = amplitudes.shape[2]
    tile_count = full_width // tile_size
    local_tiles = row_count // tile_size
    first_tile = lax.axis_index("vir") * local_tiles
    own_rows = lax.dynamic_slice_in_dim(ladder_tiles, first_tile, local_tiles, 0)
    gathered = lax.all_gather(amplitudes[0], "vir", axis=0, tiled=True)
    picked = jnp.take(
        gathered.reshape(tile_count, tile_size, tile_count, tile_size), own_rows, axis=0
    )
    factor = ladder_factor[0]
    own_factor = lax.dynamic_slice_in_dim(factor, first_tile, local_tiles, 0)
    inner_term = jnp.einsum(
        "tkac,tkcsd->stad", own_factor, picked, preferred_element_type=jnp.float32
    ).astype(jnp.bfloat16)
    inner_term = inner_term.reshape(tile_count, row_count, tile_size)
    chosen = jnp.take(inner_term, ladder_tiles, axis=0)
    ladder_sum = jnp.einsum("rkad,rkbd->rab", chosen, factor, preferred_element_type=jnp.float32)
    exchanged = lax.all_to_all(amplitudes, "pair", split_axis=1, concat_axis=0, tiled=True)
    pair_count = exchanged.shape[0]
    sub_rows = exchanged.shape[1]
    outer_count = pair_count // NJ
    positions = jnp.arange(pair_count, dtype=jnp.int32)
    inverse = jnp.zeros((pair_count,), jnp.int32).at[slab_order].set(positions)
    pair_grid = jnp.take(exchanged, inverse, axis=0)
    col_tiles = NJ * tile_count
    left_tiles = (
        pair_grid.reshape(outer_count, NJ, sub_rows, tile_count, tile_size)
        .transpose(1, 3, 2, 0, 4)
        .reshape(col_tiles, sub_rows * outer_count, tile_size)
    )
    slot_tiles = lax.all_gather(cycle_integrals, "pair", axis=0, tiled=True)
    integrals = jnp.take(slot_tiles, cycle_slots, axis=0)
    columns = jnp.take(left_tiles, cycle_tiles, axis=0)
    cycle_term = jnp.einsum(
        "tkrc,tkcb->trb", columns, integrals, preferred_element_type=jnp.float32
    ).astype(jnp.bfloat16)
    cycle_back = (
        cycle_term.reshape(NJ, tile_count, sub_rows, outer_count, tile_size)
        .transpose(3, 0, 2, 1, 4)
        .reshape(pair_count, sub_rows, full_width)
    )
    cycle_back = jnp.take(cycle_back, slab_order, axis=0)
    returned = lax.all_to_all(cycle_back, "pair", split_axis=0, concat_axis=1, tiled=True)
    summed = ladder_sum.transpose(1, 0, 2).reshape(row_count, full_width) + returned[0].astype(
        jnp.float32
    )
    mask_tiles = amp_mask[0].astype(jnp.float32)[:, None, :, None]
    masked = summed.reshape(local_tiles, tile_size, tile_count, tile_size) * mask_tiles
    return masked.reshape(1, row_count, full_width).astype(jnp.bfloat16)


def solution(mesh):
    placed = (
        P(("groups", "pair"), "vir", None),
        P("groups", None, None, None, None),
        P("groups", None),
        P(("groups", "pair"), None, None, None),
        P("groups", None),
        P("groups"),
        P("groups"),
        P(("groups", "pair"), "vir", None),
    )
    pair_count, vir_count = mesh.shape["pair"], mesh.shape["vir"]

    def per_device(*operands):
        amplitudes, factor = operands[0], operands[1]
        rows, width = amplitudes.shape[1:]
        plain = (
            amplitudes.shape[0] != 1
            or factor.shape[0] != 1
            or rows * vir_count != width
            or rows % (16 * pair_count)
            or pair_count % CORES
            or operands[3].shape[1] != vir_count
        )
        if plain:
            return on_device(*operands)
        return fused(*operands, pair_count, vir_count)

    return jax.shard_map(
        per_device,
        mesh=mesh,
        in_specs=placed,
        out_specs=P(("groups", "pair"), "vir", None),
        check_vma=False,
    )
```

```python
import functools

import jax
import jax.numpy as jnp
from jax import lax
from jax.experimental import pallas as pl
from jax.experimental.pallas import tpu as pltpu
from jax.sharding import PartitionSpec as P

NJ = 4
CORES = 2
EARLY = 3
BATCH = 2
MESH = pl.DeviceIdType.MESH


def kernel(
    pair_count,
    vir_count,
    ladder_tiles,
    cycle_tiles,
    cycle_slots,
    slab_order,
    amp_mask,
    amplitudes,
    amplitude_rows,
    factor,
    own_integrals,
    out,
    finished,
    mask_rows,
    inverse,
    pair_rows,
    row_tiles,
    integrals,
    columns,
    inner_out,
    inner_in,
    cycle_out,
    cycle_in,
    ladder_sum,
    local_sem,
    pair_sem,
    back_sem,
    vir_sem,
    inner_sem,
    near_sem,
    share_sem,
    core_sem,
    out_sem,
):
    pair = lax.axis_index("pair")
    vir = lax.axis_index("vir")
    tile = factor.shape[-1]
    kept = factor.shape[1]
    kept_cycle = own_integrals.shape[1]
    tile_count = factor.shape[0]
    local_tiles = amplitudes.shape[0]
    row_count = local_tiles * tile
    sub_rows = pair_rows.shape[1]
    own_slots = own_integrals.shape[0]
    layer_count = pair_count // CORES
    layer = pair // CORES
    core = pair % CORES
    other_core = layer * CORES + (1 - core)

    def remote(src, dst, sems, index, device):
        return pltpu.make_async_remote_copy(
            src_ref=src,
            dst_ref=dst,
            send_sem=sems.at[0, index],
            recv_sem=sems.at[1, index],
            device_id=device,
            device_id_type=MESH,
        )

    def rows_of(index):
        return pl.ds(pl.multiple_of(index * sub_rows, 16), sub_rows)

    def block_of(index):
        return pl.ds(pl.multiple_of(index * row_count, tile), row_count)

    def tile_at(index):
        return pl.ds(pl.multiple_of(index * tile, tile), tile)

    def slots_of(index):
        return pl.ds(index * own_slots, own_slots)

    def tiles_of(index):
        return pl.ds(index * local_tiles, local_tiles)

    barrier = pltpu.get_barrier_semaphore()
    for step in range(1, pair_count):
        pl.semaphore_signal(
            barrier, inc=1, device_id={"pair": (pair + step) % pair_count}, device_id_type=MESH
        )
    for step in range(1, vir_count):
        pl.semaphore_signal(
            barrier, inc=1, device_id={"vir": (vir + step) % vir_count}, device_id_type=MESH
        )
    pl.semaphore_wait(barrier, pair_count + vir_count - 2)

    near = []
    for step in range(1, layer_count):
        peer = ((layer + step) % layer_count) * CORES + core
        copy = remote(
            own_integrals.at[:, vir],
            integrals.at[slots_of(pair), vir],
            near_sem,
            step,
            {"pair": peer},
        )
        copy.start()
        near.append(copy)
    across = []
    copy = remote(
        own_integrals, integrals.at[slots_of(pair)], core_sem, 0, {"pair": other_core}
    )
    copy.start()
    across.append(copy)
    local = [
        pltpu.make_async_copy(own_integrals, integrals.at[slots_of(pair)], local_sem.at[0]),
        pltpu.make_async_copy(
            amplitudes.at[:, :, block_of(vir)], columns.at[tiles_of(vir)], local_sem.at[1]
        ),
        pltpu.make_async_copy(
            amplitude_rows.at[rows_of(pair), :], pair_rows.at[pair], local_sem.at[2]
        ),
    ]
    for copy in local:
        copy.start()

    crossing = []
    for step in range(1, vir_count):
        peer = (vir + step) % vir_count
        copy = remote(
            amplitudes.at[:, :, block_of(peer)],
            columns.at[tiles_of(vir)],
            vir_sem,
            step,
            {"vir": peer},
        )
        crossing.append(copy)
    order = sorted(range(1, pair_count), key=lambda step: -min(step, pair_count - step))
    forward = []
    for step in order:
        peer = (pair + step) % pair_count
        copy = remote(
            amplitude_rows.at[rows_of(peer), :], pair_rows.at[pair], pair_sem, step, {"pair": peer}
        )
        forward.append(copy)
    for copy in crossing[:EARLY]:
        copy.start()

    for flat in range(pair_count):
        held = 0
        for row in range(pair_count):
            held = jnp.where(slab_order[row] == flat, row, held)
        inverse[flat] = held
    for row in range(local_tiles):
        for index in range(tile_count):
            mask_rows[row : row + 1, index * tile : (index + 1) * tile] = jnp.full(
                (1, tile), amp_mask[row, index].astype(jnp.float32)
            )

    def source_of(step):
        return ((layer + layer_count - step) % layer_count) * CORES + core

    def share(source, kept_index, sems, index, device):
        place = integrals.at[slots_of(source), kept_index]
        copy = remote(place, place, sems, index, device)
        copy.start()
        return copy

    shared = []
    for step in range(1, layer_count):
        near[step - 1].wait_recv()
        source = source_of(step)
        for hop in range(1, vir_count):
            shared.append(
                share(
                    source,
                    vir,
                    share_sem,
                    step * vir_count + hop,
                    {"vir": (vir + hop) % vir_count},
                )
            )
        across.append(share(source, vir, core_sem, step * vir_count, {"pair": other_core}))
        for copy in forward[(step - 1) * BATCH : step * BATCH if step < layer_count - 1 else None]:
            copy.start()
    for copy in crossing[EARLY:]:
        copy.start()

    for copy in crossing:
        copy.wait_recv()
    local[1].wait()

    def inner_step(owner, index):
        row_tile = owner * local_tiles + index
        left = jnp.concatenate([factor[row_tile, k] for k in range(kept)], axis=1)
        right = jnp.concatenate(
            [columns[ladder_tiles[k, row_tile]] for k in range(kept)], axis=0
        )
        value = jnp.dot(left, right, preferred_element_type=jnp.float32).astype(jnp.bfloat16)
        for part in range(local_tiles):
            inner_out[owner, part, tile_at(index), :] = value[:, part * tile : (part + 1) * tile]

    inner_sends = []
    for step in list(range(1, vir_count)) + [0]:
        peer = (vir + step) % vir_count

        @pl.loop(0, local_tiles)
        def _(index):
            inner_step(peer, index)

        if step:
            copy = remote(
                inner_out.at[peer], inner_in.at[tiles_of(vir)], inner_sem, step, {"vir": peer}
            )
            copy.start()
            inner_sends.append(copy)
        else:
            own_inner = pltpu.make_async_copy(
                inner_out.at[peer], inner_in.at[tiles_of(vir)], local_sem.at[3]
            )
            own_inner.start()

    for step in range(1, layer_count):
        for hop in range(1, vir_count):
            shared[(step - 1) * (vir_count - 1) + hop - 1].wait_recv()
            across.append(
                share(
                    source_of(step),
                    (vir + vir_count - hop) % vir_count,
                    core_sem,
                    step * vir_count + hop,
                    {"pair": other_core},
                )
            )

    def split_columns(source):
        for index in range(tile_count):
            row_tiles[source * tile_count + index] = pair_rows[
                source, :, index * tile : (index + 1) * tile
            ]

    local[0].wait()
    local[2].wait()
    split_columns(pair)
    for step, copy in zip(order, forward):
        copy.wait_recv()
        split_columns((pair + pair_count - step) % pair_count)
    for copy in across:
        copy.wait_recv()

    def cycle_step(peer, index):
        flat = slab_order[peer]
        outer = lax.div(flat, NJ)
        column = lax.rem(flat, NJ) * tile_count + index
        pieces = []
        for k in range(kept_cycle):
            row_tile = cycle_tiles[k, column]
            held = inverse[outer * NJ + lax.div(row_tile, tile_count)]
            pieces.append(row_tiles[held * tile_count + lax.rem(row_tile, tile_count)])
        left = jnp.concatenate(pieces, axis=1)
        right = integrals[cycle_slots[column]].reshape(kept_cycle * tile, tile)
        value = jnp.dot(left, right, preferred_element_type=jnp.float32)
        cycle_out[peer, :, tile_at(index)] = value.astype(jnp.bfloat16)

    back = []
    for step in order + [0]:
        peer = (pair + step) % pair_count

        @pl.loop(0, tile_count)
        def _(index):
            cycle_step(peer, index)

        if step:
            copy = remote(
                cycle_out.at[peer], cycle_in.at[rows_of(pair), :], back_sem, step, {"pair": peer}
            )
            copy.start()
            back.append(copy)
        else:
            own_back = pltpu.make_async_copy(
                cycle_out.at[peer], cycle_in.at[rows_of(pair), :], local_sem.at[4]
            )
            own_back.start()

    for copy in inner_sends:
        copy.wait_recv()
    own_inner.wait()

    @pl.loop(0, tile_count)
    def _(index):
        left = jnp.concatenate([inner_in[ladder_tiles[k, index]] for k in range(kept)], axis=1)
        right = jnp.concatenate([factor[index, k] for k in range(kept)], axis=1)
        ladder_sum[:, tile_at(index)] = lax.dot_general(
            left, right, (((1,), (1,)), ((), ())), preferred_element_type=jnp.float32
        )

    stores = []

    def finish(source):
        for part in range(sub_rows // 16):
            row = source * sub_rows + part * 16
            rows = pl.ds(pl.multiple_of(row, 16), 16)
            total = ladder_sum[rows, :] + cycle_in[rows, :].astype(jnp.float32)
            finished[rows, :] = (mask_rows[pl.ds(row // tile, 1), :] * total).astype(jnp.bfloat16)
        copy = pltpu.make_async_copy(
            finished.at[rows_of(source), :], out.at[rows_of(source), :], out_sem.at[len(stores)]
        )
        copy.start()
        stores.append(copy)

    own_back.wait()
    finish(pair)
    for step, copy in sorted(
        zip(order, back), key=lambda item: item[0] not in (1, pair_count - 1)
    ):
        copy.wait_recv()
        finish((pair + pair_count - step) % pair_count)
    for copy in stores:
        copy.wait()
    for copy in near + crossing + forward + across + shared + inner_sends + back:
        copy.wait_send()


def fused(
    amplitudes,
    ladder_factor,
    ladder_tiles,
    cycle_integrals,
    cycle_tiles,
    cycle_slots,
    slab_order,
    amp_mask,
    pair_count,
    vir_count,
):
    tile = ladder_factor.shape[-1]
    _, row_count, full_width = amplitudes.shape
    tile_count = full_width // tile
    sub_rows = row_count // pair_count
    own_slots, kept_cycle = cycle_integrals.shape[:2]
    smem = pl.BlockSpec(memory_space=pltpu.SMEM)
    vmem = pl.BlockSpec(memory_space=pltpu.VMEM)
    hbm = pl.BlockSpec(memory_space=pl.ANY)
    layer_count = pair_count // CORES

    def sems(count):
        return pltpu.SemaphoreType.DMA((2, count))

    result = pl.pallas_call(
        functools.partial(kernel, pair_count, vir_count),
        out_shape=jax.ShapeDtypeStruct((row_count, full_width), jnp.bfloat16),
        in_specs=[smem] * 5 + [hbm, hbm, vmem, hbm],
        out_specs=hbm,
        scratch_shapes=[
            pltpu.VMEM((row_count, full_width), jnp.bfloat16),
            pltpu.VMEM((row_count // tile, full_width), jnp.float32),
            pltpu.SMEM((pair_count,), jnp.int32),
            pltpu.VMEM((pair_count, sub_rows, full_width), jnp.bfloat16),
            pltpu.VMEM((pair_count * tile_count, sub_rows, tile), jnp.bfloat16),
            pltpu.VMEM((own_slots * pair_count, kept_cycle, tile, tile), jnp.bfloat16),
            pltpu.VMEM((tile_count, tile, row_count), jnp.bfloat16),
            pltpu.VMEM((vir_count, row_count // tile, row_count, tile), jnp.bfloat16),
            pltpu.VMEM((tile_count, row_count, tile), jnp.bfloat16),
            pltpu.VMEM((pair_count, sub_rows, full_width), jnp.bfloat16),
            pltpu.VMEM((row_count, full_width), jnp.bfloat16),
            pltpu.VMEM((row_count, full_width), jnp.float32),
            pltpu.SemaphoreType.DMA((5,)),
            sems(pair_count),
            sems(pair_count),
            sems(vir_count),
            sems(vir_count),
            sems(layer_count),
            sems(layer_count * vir_count),
            sems(layer_count * vir_count),
            pltpu.SemaphoreType.DMA((pair_count,)),
        ],
        compiler_params=pltpu.CompilerParams(
            collective_id=0, has_side_effects=True, vmem_limit_bytes=56 * 1024 * 1024
        ),
    )(
        ladder_tiles.T,
        cycle_tiles.T,
        cycle_slots,
        slab_order,
        amp_mask[0],
        amplitudes.reshape(row_count // tile, tile, full_width),
        amplitudes[0],
        ladder_factor[0],
        cycle_integrals,
    )
    return result[None]


def on_device(
    amplitudes,
    ladder_factor,
    ladder_tiles,
    cycle_integrals,
    cycle_tiles,
    cycle_slots,
    slab_order,
    amp_mask,
):
    tile_size = ladder_factor.shape[-1]
    row_count = amplitudes.shape[1]
    full_width = amplitudes.shape[2]
    tile_count = full_width // tile_size
    local_tiles = row_count // tile_size
    first_tile = lax.axis_index("vir") * local_tiles
    own_rows = lax.dynamic_slice_in_dim(ladder_tiles, first_tile, local_tiles, 0)
    gathered = lax.all_gather(amplitudes[0], "vir", axis=0, tiled=True)
    picked = jnp.take(
        gathered.reshape(tile_count, tile_size, tile_count, tile_size), own_rows, axis=0
    )
    factor = ladder_factor[0]
    own_factor = lax.dynamic_slice_in_dim(factor, first_tile, local_tiles, 0)
    inner_term = jnp.einsum(
        "tkac,tkcsd->stad", own_factor, picked, preferred_element_type=jnp.float32
    ).astype(jnp.bfloat16)
    inner_term = inner_term.reshape(tile_count, row_count, tile_size)
    chosen = jnp.take(inner_term, ladder_tiles, axis=0)
    ladder_sum = jnp.einsum("rkad,rkbd->rab", chosen, factor, preferred_element_type=jnp.float32)
    exchanged = lax.all_to_all(amplitudes, "pair", split_axis=1, concat_axis=0, tiled=True)
    pair_count = exchanged.shape[0]
    sub_rows = exchanged.shape[1]
    outer_count = pair_count // NJ
    positions = jnp.arange(pair_count, dtype=jnp.int32)
    inverse = jnp.zeros((pair_count,), jnp.int32).at[slab_order].set(positions)
    pair_grid = jnp.take(exchanged, inverse, axis=0)
    col_tiles = NJ * tile_count
    left_tiles = (
        pair_grid.reshape(outer_count, NJ, sub_rows, tile_count, tile_size)
        .transpose(1, 3, 2, 0, 4)
        .reshape(col_tiles, sub_rows * outer_count, tile_size)
    )
    slot_tiles = lax.all_gather(cycle_integrals, "pair", axis=0, tiled=True)
    integrals = jnp.take(slot_tiles, cycle_slots, axis=0)
    columns = jnp.take(left_tiles, cycle_tiles, axis=0)
    cycle_term = jnp.einsum(
        "tkrc,tkcb->trb", columns, integrals, preferred_element_type=jnp.float32
    ).astype(jnp.bfloat16)
    cycle_back = (
        cycle_term.reshape(NJ, tile_count, sub_rows, outer_count, tile_size)
        .transpose(3, 0, 2, 1, 4)
        .reshape(pair_count, sub_rows, full_width)
    )
    cycle_back = jnp.take(cycle_back, slab_order, axis=0)
    returned = lax.all_to_all(cycle_back, "pair", split_axis=0, concat_axis=1, tiled=True)
    summed = ladder_sum.transpose(1, 0, 2).reshape(row_count, full_width) + returned[0].astype(
        jnp.float32
    )
    mask_tiles = amp_mask[0].astype(jnp.float32)[:, None, :, None]
    masked = summed.reshape(local_tiles, tile_size, tile_count, tile_size) * mask_tiles
    return masked.reshape(1, row_count, full_width).astype(jnp.bfloat16)


def solution(mesh):
    placed = (
        P(("groups", "pair"), "vir", None),
        P("groups", None, None, None, None),
        P("groups", None),
        P(("groups", "pair"), None, None, None),
        P("groups", None),
        P("groups"),
        P("groups"),
        P(("groups", "pair"), "vir", None),
    )
    pair_count, vir_count = mesh.shape["pair"], mesh.shape["vir"]

    def per_device(*operands):
        amplitudes, factor = operands[0], operands[1]
        rows, width = amplitudes.shape[1:]
        plain = (
            amplitudes.shape[0] != 1
            or factor.shape[0] != 1
            or rows * vir_count != width
            or rows % (16 * pair_count)
            or pair_count % CORES
            or operands[3].shape[1] != vir_count
        )
        if plain:
            return on_device(*operands)
        return fused(*operands, pair_count, vir_count)

    return jax.shard_map(
        per_device,
        mesh=mesh,
        in_specs=placed,
        out_specs=P(("groups", "pair"), "vir", None),
        check_vma=False,
    )
```
